32 devices in a mesh: rows: 8 (over y, x, core), cols: 4 (over z).
Axes of the slice: x: 2, y: 2, z: 4, core: 2. Of those that a mesh axis runs over, the one named last changes fastest.
Arguments:
- tokens: bfloat16 [32768, 1024], P('rows', 'cols'), may hold values from -6 to 6
- qkv_weight: bfloat16 [1024, 4096], P('rows', 'cols'), may hold values from -0.1875 to 0.1875
- out_weight: bfloat16 [2048, 1024], P('cols', 'rows'), may hold values from -1 to 1
- expand_weight: bfloat16 [1024, 2, 3072], P('rows', None, 'cols'), may hold values from -0.1875 to 0.1875
- down_weight: bfloat16 [3072, 1024], P('cols', 'rows'), may hold values from -0.109375 to 0.109375
- attn_gain: float32 [1024], replicated, may hold values from 0.1 to 1.9
- mlp_gain: float32 [1024], replicated, may hold values from 0.1 to 1.9
- query_gain: float32 [128], replicated, may hold values from 0.1 to 1.9
- key_gain: float32 [128], replicated, may hold values from 0.1 to 1.9
- segment_ids: int32 [8, 4096], P('rows'), may hold values from 0 to 3, never falling along the last dimension, each value on 1 to 2048 neighbouring positions
- cotangent: bfloat16 [32768, 1024], P('rows', 'cols'), may hold values from -6 to 6
Outputs:
- output: bfloat16 [32768, 1024], P('rows', 'cols')
- input_grad: float32 [32768, 1024], P('rows', 'cols')
- qkv_grad: float32 [1024, 4096], P('rows', 'cols')
- out_grad: float32 [2048, 1024], P('cols', 'rows')
- expand_grad: float32 [1024, 2, 3072], P('rows', None, 'cols')
- down_grad: float32 [3072, 1024], P('cols', 'rows')
- attn_gain_grad: float32 [1024], replicated
- mlp_gain_grad: float32 [1024], replicated
- query_gain_grad: float32 [128], replicated
- key_gain_grad: float32 [128], replicated
The draws below stay inside these ranges and needn't reach their ends.
Inputs may be any that keep to these rules, and one draw needn't show every extreme that they name: `segment_ids`: within a sequence the document numbers never fall, every number from 0 to 3 appears, each document has at most 2048 tokens and one has exactly that many.
All inputs are finite; a program needn't handle non-finite values.
Results may differ from the reference program's by a relative error of at most 0.013.
Values may be sent and summed in bfloat16 or wider, within the bound.
A program may use at most 512 MiB of HBM per device.

```python
import math
import jax
import jax.numpy as jnp
import numpy as np
from jax import lax

D = 1024
FF = 3072
HEADS = 16
KV_HEADS = 8
HEAD = 128
SEQ_LEN = 4096
DOCS = 4
SEQS = 8
TOKENS = 32768


def steps_of(stream_key, extent, cuts, least, high):
    level = 1.0
    for dim, blocks in cuts:
        draws = jax.random.uniform(jax.random.fold_in(jax.random.fold_in(stream_key, 6), dim), (blocks,), jnp.float32, least / len(cuts), high / len(cuts))
        level = level * jnp.repeat(jnp.exp(draws), extent[dim] // blocks).reshape((-1,) + (1,) * (len(extent) - 1 - dim))
    return level


def profile(number_of, total, bound, lean):
    portions = [(1 << 20) // math.isqrt(grade ** lean) + 1 for grade in range(2, number_of + 1)]
    spare, holding = total - bound - (number_of - 1), [1] * (number_of - 1)
    while spare > 0:
        candidates = [i for i in range(number_of - 1) if holding[i] < bound]
        pool, remaining = sum([portions[i] for i in candidates]), spare
        for i in candidates:
            more = min(bound - holding[i], max(1, remaining * portions[i] // pool), spare)
            holding[i] = holding[i] + more
            spare = spare - more
    return np.array([bound] + holding)


def uneven(own_key, amount, total, bound, lean):
    if amount == 2:
        one = jax.random.randint(own_key, (), max(1, total - bound), min(bound, total - 1) + 1)
        return jnp.stack([one, total - one])
    lengths = jnp.asarray(profile(amount, total, bound, lean), jnp.int32)
    couples = (amount - 1) // 2
    donor, sink = lengths[1:1 + 2 * couples:2], lengths[2:2 + 2 * couples:2]
    slack = jnp.minimum(donor - 1, bound - sink)
    passed = jax.random.randint(jax.random.fold_in(own_key, 1), (couples,), 0, 1 << 20) % (slack + 1)
    lengths = lengths.at[1:1 + 2 * couples:2].set(donor - passed).at[2:2 + 2 * couples:2].set(sink + passed)
    return lengths[jax.random.permutation(jax.random.fold_in(own_key, 2), amount)]


def scatter_about(rng, dims, deviation, limit, cuts=(), kind=jnp.bfloat16):
    loudness = steps_of(rng, dims, cuts, -0.22, 0.18) if cuts else 1.0
    values = jax.random.normal(rng, dims, jnp.float32) * deviation * loudness
    return jnp.minimum(jnp.maximum(values, -limit), limit).astype(kind)


def setup_inputs(seed: int = 0) -> dict:
    splits = jax.random.split(jax.random.key(seed), 12)
    return {
        "tokens": scatter_about(splits[0], (TOKENS, D), 1.0, 6.0, ((0, 8), (1, 4))),
        "qkv_weight": scatter_about(splits[1], (D, (HEADS + 2 * KV_HEADS) * HEAD), D ** -0.5, 0.1875, ((0, 8), (1, 4))),
        "out_weight": scatter_about(splits[2], (HEADS * HEAD, D), (HEADS * HEAD // 64) ** -0.5, 1.0, ((0, 4), (1, 8))),
        "expand_weight": scatter_about(splits[3], (D, 2, FF), D ** -0.5, 0.1875, ((0, 8), (2, 4))),
        "down_weight": scatter_about(splits[4], (FF, D), FF ** -0.5, 0.109375, ((0, 4), (1, 8))),
        "attn_gain": jnp.clip(1.0 + 0.18 * jax.random.normal(splits[5], (D,), jnp.float32), 0.1, 1.9),
        "mlp_gain": jnp.clip(1.0 + 0.18 * jax.random.normal(splits[6], (D,), jnp.float32), 0.1, 1.9),
        "query_gain": jnp.clip(1.0 + 0.18 * jax.random.normal(splits[7], (HEAD,), jnp.float32), 0.1, 1.9),
        "key_gain": jnp.clip(1.0 + 0.18 * jax.random.normal(splits[8], (HEAD,), jnp.float32), 0.1, 1.9),
        "segment_ids": jax.vmap(lambda own: jnp.searchsorted(jnp.cumsum(uneven(own, DOCS, SEQ_LEN, SEQ_LEN // 2, 0)), jnp.arange(SEQ_LEN), side="right"))(jax.random.split(splits[9], SEQS)).reshape((SEQS, SEQ_LEN)).astype(jnp.int32),
        "cotangent": scatter_about(splits[10], (TOKENS, D), 1.0, 6.0, ((0, 8), (1, 4))),
    }


EPS = 1e-06
THETA = 1000000.0

@jax.custom_vjp
def low(v):
    return lax.optimization_barrier(v.astype(jnp.bfloat16)).astype(jnp.float32)

@jax.custom_vjp
def low_back(v):
    return v

def low_keep(v):
    return (low(v), None)

def low_pass(kept, grad):
    return (grad,)

def back_keep(v):
    return (v, None)

def back_low(kept, grad):
    return (low(grad),)
low.defvjp(low_keep, low_pass)
low_back.defvjp(back_keep, back_low)

def exact_dot(left, right):
    return jnp.dot(left, right, precision=lax.Precision.HIGHEST, preferred_element_type=jnp.float32)

def rms_norm(values, scaling):
    return values * lax.rsqrt(lax.optimization_barrier(jnp.mean(values * values, axis=-1, keepdims=True)) + EPS) * scaling

def rotate(values, cosine, sine_table):
    half_size = values.shape[-1] // 2
    front = values[..., :half_size]
    back_half = values[..., half_size:]
    return jnp.concatenate([front * cosine - back_half * sine_table, back_half * cosine + front * sine_table], axis=-1)

def rope_tables(segment):
    length = segment.shape[0]
    member = segment[:, None] == jnp.arange(DOCS, dtype=jnp.int32)[None, :]
    doc_sizes = lax.optimization_barrier(jnp.sum(member.astype(jnp.int32), axis=0, dtype=jnp.int32))
    starts = jnp.cumsum(doc_sizes, dtype=jnp.int32) - doc_sizes
    doc_start = lax.optimization_barrier(jnp.sum(jnp.where(member, starts[None, :], 0), axis=1, dtype=jnp.int32))
    position = (jnp.arange(length, dtype=jnp.int32) - doc_start).astype(jnp.float32)
    frequency = THETA ** (-jnp.arange(0, HEAD, 2, dtype=jnp.float32) / HEAD)
    angles = position[:, None] * frequency[None, :]
    return (jnp.cos(angles), jnp.sin(angles))

def layer(tokens, qkv_weight, out_weight, expand_weight, down_weight, attn_gain, mlp_gain, query_gain, key_gain, segment):
    length = tokens.shape[0]
    per_group = HEADS // KV_HEADS
    cosine, sine_table = rope_tables(segment)
    normed = low(rms_norm(tokens, attn_gain))
    grouped = low_back(exact_dot(normed, qkv_weight)).reshape(length, KV_HEADS, per_group + 2, HEAD)
    queries = low(rotate(rms_norm(grouped[:, :, :per_group], query_gain), cosine[:, None, None], sine_table[:, None, None]))
    keys = low(rotate(rms_norm(grouped[:, :, per_group], key_gain), cosine[:, None], sine_table[:, None]))
    values = low(grouped[:, :, per_group + 1])
    scores = low_back(jnp.einsum('qhgd,khd->hgqk', queries, keys, precision=lax.Precision.HIGHEST) * HEAD ** (-0.5))
    places = jnp.arange(length, dtype=jnp.int32)
    allowed = (segment[:, None] == segment[None, :]) & (places[:, None] >= places[None, :])
    scores = jnp.where(allowed, scores, -1e+30)
    chances = low(jax.nn.softmax(scores, axis=-1))
    mixed = jnp.einsum('hgqk,khd->qhgd', chances, values, precision=lax.Precision.HIGHEST)
    mixed = low(low_back(mixed)).reshape(length, HEADS * HEAD)
    hidden = tokens + low_back(exact_dot(mixed, out_weight))
    normed_two = low(rms_norm(hidden, mlp_gain))
    gate_up = low_back(jnp.einsum('td,dsf->tsf', normed_two, expand_weight, precision=lax.Precision.HIGHEST))
    activation = low(jax.nn.silu(gate_up[:, 0]) * gate_up[:, 1])
    return hidden + low_back(exact_dot(activation, down_weight))

def reference(tokens, qkv_weight, out_weight, expand_weight, down_weight, attn_gain, mlp_gain, query_gain, key_gain, segment_ids, cotangent):
    params = tuple((weight.astype(jnp.float32) for weight in (qkv_weight, out_weight, expand_weight, down_weight, attn_gain, mlp_gain, query_gain, key_gain)))
    token_rows = tokens.astype(jnp.float32).reshape(SEQS, SEQ_LEN, D)
    cotan_rows = cotangent.astype(jnp.float32).reshape(SEQS, SEQ_LEN, D)

    def step_one(running, inputs_row):
        sequence, segment, gradient = inputs_row

        def forward_seq(seq_tokens, *weights):
            return layer(seq_tokens, *weights, segment)
        result, pullback = jax.vjp(forward_seq, sequence, *params)
        pieces = pullback(gradient)
        running = jax.tree.map(lambda first_val, second_val: first_val + second_val, running, tuple(pieces[1:]))
        return (running, (result.astype(jnp.bfloat16), pieces[0]))
    zeros_start = tuple((jnp.zeros_like(weight) for weight in params))
    totals, (outputs, input_grads) = lax.scan(step_one, zeros_start, (token_rows, segment_ids, cotan_rows))
    return (outputs.reshape(TOKENS, D), input_grads.reshape(TOKENS, D), totals[0], totals[1], totals[2], totals[3], totals[4], totals[5], totals[6], totals[7])
```

```python
from functools import partial

import jax
import jax.numpy as jnp
from jax import lax
from jax.experimental import pallas as pl
from jax.experimental.pallas import tpu as pltpu
from jax.sharding import PartitionSpec as P

HEADS = 16
KV_HEADS = 8
HEAD = 128
DOCS = 4
PER = HEADS // KV_HEADS
WIDTH = (PER + 2) * HEAD

EPS = 1e-06
THETA = 1000000.0
LOG2E = 1.4426950408889634
SCALE = HEAD ** (-0.5)
BLOCK = 512
F32 = jnp.float32
BF16 = jnp.bfloat16


def dot(a, b, ca, cb):
    return lax.dot_general(a, b, (((ca,), (cb,)), ((), ())), preferred_element_type=F32)


def forward_kernel(lo, full, qk_ref, k_ref, v_ref, start_ref, o_ref, lse_ref, vext, acc):
    i = pl.program_id(1)
    block = qk_ref.shape[0]

    @pl.when(i == 0)
    def _():
        vext[:, :HEAD] = v_ref[...]
        vext[:, HEAD:] = jnp.ones((vext.shape[0], HEAD), BF16)

    acc[...] = jnp.zeros_like(acc)

    def step(j, masked):
        at = pl.ds(pl.multiple_of(j * block, block), block)
        keys = k_ref[at, :]
        vals = vext[at, :]
        if masked:
            place = lax.broadcasted_iota(jnp.int32, (block, block), 1) + j * block
            query = lax.broadcasted_iota(jnp.int32, (block, block), 0) + i * block
            keep = (place >= start_ref[:, :1]) & (place <= query)
        for h in range(PER):
            s = dot(qk_ref[:, h * HEAD : (h + 1) * HEAD], keys, 1, 1)
            p = jnp.exp2(s * (SCALE * LOG2E))
            if masked:
                p = jnp.where(keep, p, 0.0)
            acc[h] += dot(p.astype(BF16), vals, 1, 0)

    first = jnp.minimum(full[i], i)

    @pl.loop(lo[i], first)
    def _(j):
        step(j, True)

    @pl.loop(first, i)
    def _(j):
        step(j, False)

    step(i, True)
    for h in range(PER):
        total = acc[h, :, HEAD:]
        o_ref[:, h * HEAD : (h + 1) * HEAD] = (acc[h, :, :HEAD] / total).astype(BF16)
        lse_ref[h] = jnp.transpose(jnp.log2(total))[:8]


def backward_kernel(
    last, full, q_ref, k_ref, v_ref, do_ref, o_ref, lse_ref, start_ref, out_ref, dq, inner, dk, dv
):
    j = pl.program_id(1)
    block = k_ref.shape[0]
    steps = pl.num_programs(1)

    @pl.when(j == 0)
    def _():
        dq[...] = jnp.zeros_like(dq)

        @pl.loop(0, steps)
        def _(i):
            at = pl.ds(pl.multiple_of(i * block, block), block)
            for h in range(PER):
                cols = slice(h * HEAD, (h + 1) * HEAD)
                term = do_ref[at, cols].astype(F32) * o_ref[at, cols].astype(F32)
                row = jnp.sum(term, axis=1, keepdims=True)
                inner[h, :, at] = jnp.transpose(jnp.broadcast_to(row, (block, HEAD)))[:8]

    dk[...] = jnp.zeros_like(dk)
    dv[...] = jnp.zeros_like(dv)
    keys = k_ref[...]
    vals = v_ref[...]

    def step(i, masked):
        at = pl.ds(pl.multiple_of(i * block, block), block)
        if masked:
            place = lax.broadcasted_iota(jnp.int32, (block, block), 0) + j * block
            query = lax.broadcasted_iota(jnp.int32, (block, block), 1) + i * block
            keep = (place >= start_ref[:1, at]) & (place <= query)
        for h in range(PER):
            cols = slice(h * HEAD, (h + 1) * HEAD)
            q = q_ref[at, cols]
            do = do_ref[at, cols]
            s = dot(keys, q, 1, 1)
            p = jnp.exp2(s * (SCALE * LOG2E) - lse_ref[h, :1, at])
            if masked:
                p = jnp.where(keep, p, 0.0)
            dp = dot(vals, do, 1, 1)
            ds = (p * (dp - inner[h, :1, at])).astype(BF16)
            dv[...] += dot(p.astype(BF16), do, 1, 0)
            dk[...] += dot(ds, q, 1, 0)
            dq[at, cols] += dot(ds, keys, 0, 0)

    step(j, True)
    middle = jnp.maximum(full[j], j) + 1

    @pl.loop(j + 1, middle)
    def _(i):
        step(i, False)

    @pl.loop(middle, last[j] + 1)
    def _(i):
        step(i, True)

    here = pl.ds(pl.multiple_of(j * block, block), block)
    out_ref[here, PER * HEAD : (PER + 1) * HEAD] = (dk[...] * SCALE).astype(BF16)
    out_ref[here, (PER + 1) * HEAD :] = dv[...].astype(BF16)

    @pl.when(j == steps - 1)
    def _():
        out_ref[:, : PER * HEAD] = (dq[...] * SCALE).astype(BF16)


def attend(qkv, start, block):
    length, width = qkv.shape
    groups = width // WIDTH
    steps = length // block
    blocked = start.reshape(steps, block)
    lo = blocked[:, 0] // block
    full = (blocked[:, -1] + block - 1) // block
    wide = jnp.broadcast_to(start[:, None], (length, HEAD))
    return pl.pallas_call(
        forward_kernel,
        grid_spec=pltpu.PrefetchScalarGridSpec(
            num_scalar_prefetch=2,
            grid=(groups, steps),
            in_specs=[
                pl.BlockSpec((block, PER * HEAD), lambda g, i, *_: (i, g * 2)),
                pl.BlockSpec((length, HEAD), lambda g, i, *_: (0, g * 4 + 2)),
                pl.BlockSpec((length, HEAD), lambda g, i, *_: (0, g * 4 + 3)),
                pl.BlockSpec((block, HEAD), lambda g, i, *_: (i, 0)),
            ],
            out_specs=[
                pl.BlockSpec((block, PER * HEAD), lambda g, i, *_: (i, g)),
                pl.BlockSpec((PER, 8, block), lambda g, i, *_: (g, 0, i)),
            ],
            scratch_shapes=[
                pltpu.VMEM((length, 2 * HEAD), BF16),
                pltpu.VMEM((PER, block, 2 * HEAD), F32),
            ],
        ),
        out_shape=[
            jax.ShapeDtypeStruct((length, groups * PER * HEAD), BF16),
            jax.ShapeDtypeStruct((groups * PER, 8, length), F32),
        ],
        compiler_params=pltpu.CompilerParams(vmem_limit_bytes=40 * 2**20),
        cost_estimate=pl.CostEstimate(
            flops=groups * PER * length * length * HEAD * 4,
            bytes_accessed=length * width * 4,
            transcendentals=groups * PER * length * length // 2,
        ),
        name="attend",
    )(lo, full, qkv, qkv, qkv, wide)


def attend_back(qkv, mixed, lse, grad, start, block):
    length, width = qkv.shape
    groups = width // WIDTH
    steps = length // block
    blocked = start.reshape(steps, block)
    index = jnp.arange(steps, dtype=jnp.int32)
    last = jnp.sum((blocked[:, 0] // block)[None, :] <= index[:, None], axis=1, dtype=jnp.int32) - 1
    full = jnp.sum(blocked[:, -1][None, :] <= (index * block)[:, None], axis=1, dtype=jnp.int32) - 1
    wide = jnp.broadcast_to(start[None, :], (8, length))
    return pl.pallas_call(
        backward_kernel,
        grid_spec=pltpu.PrefetchScalarGridSpec(
            num_scalar_prefetch=2,
            grid=(groups, steps),
            in_specs=[
                pl.BlockSpec((length, PER * HEAD), lambda g, j, *_: (0, g * 2)),
                pl.BlockSpec((block, HEAD), lambda g, j, *_: (j, g * 4 + 2)),
                pl.BlockSpec((block, HEAD), lambda g, j, *_: (j, g * 4 + 3)),
                pl.BlockSpec((length, PER * HEAD), lambda g, j, *_: (0, g)),
                pl.BlockSpec((length, PER * HEAD), lambda g, j, *_: (0, g)),
                pl.BlockSpec((PER, 8, length), lambda g, j, *_: (g, 0, 0)),
                pl.BlockSpec((8, length), lambda g, j, *_: (0, 0)),
            ],
            out_specs=pl.BlockSpec((length, WIDTH), lambda g, j, *_: (0, g)),
            scratch_shapes=[
                pltpu.VMEM((length, PER * HEAD), F32),
                pltpu.VMEM((PER, 8, length), F32),
                pltpu.VMEM((block, HEAD), F32),
                pltpu.VMEM((block, HEAD), F32),
            ],
        ),
        out_shape=jax.ShapeDtypeStruct((length, width), BF16),
        compiler_params=pltpu.CompilerParams(vmem_limit_bytes=48 * 2**20),
        cost_estimate=pl.CostEstimate(
            flops=groups * PER * length * length * HEAD * 10,
            bytes_accessed=length * width * 8,
            transcendentals=groups * PER * length * length // 2,
        ),
        name="attend_back",
    )(last, full, qkv, qkv, qkv, grad, mixed, lse, wide)


def rotate(values, cosine, sine_table):
    half_size = values.shape[-1] // 2
    front = values[..., :half_size]
    back_half = values[..., half_size:]
    return jnp.concatenate(
        [front * cosine - back_half * sine_table, back_half * cosine + front * sine_table], axis=-1
    )


def head_norm(values, scaling):
    return values * lax.rsqrt(jnp.mean(values * values, axis=-1, keepdims=True) + EPS) * scaling


def heads_local(query_raw, key_raw, query_gain, key_gain, cosine, sine_table):
    queries = rotate(
        head_norm(query_raw, query_gain), cosine[:, None, None], sine_table[:, None, None]
    )
    keys = rotate(head_norm(key_raw, key_gain), cosine[:, None], sine_table[:, None])
    return (queries, keys)


def norm_scale(values):
    return lax.rsqrt(jnp.mean(values * values, axis=1, keepdims=True) + EPS)


def norm_backward(values, scale, scaling, gradient):
    inner_sum = jnp.mean(gradient * scaling * values, axis=1, keepdims=True)
    back_grad = scale * scaling * gradient - values * scale * scale * scale * inner_sum
    gain_part = jnp.sum(gradient * values * scale, axis=0)
    return (back_grad, gain_part)


def local(
    tokens,
    qkv_weight,
    out_weight,
    expand_weight,
    down_weight,
    attn_gain,
    mlp_gain,
    query_gain,
    key_gain,
    segment_ids,
    cotangent,
):
    rows = lax.axis_size("rows")
    cols = lax.axis_size("cols")
    length, local_width = tokens.shape
    width = local_width * cols
    paired = cols == 4 and rows % 2 == 0
    share = 2 if paired else cols // 2
    count = length // cols
    if paired:
        team_axis = "rows"
        team_sets = [[2 * i, 2 * i + 1] for i in range(rows // 2)]
        seat = lax.axis_index("rows") % 2
    else:
        team_axis = "cols"
        team_sets = [[share * i + k for k in range(share)] for i in range(2)]
        seat = lax.axis_index("cols") % share

    def team(values, split, concat):
        return lax.all_to_all(values, team_axis, split, concat, axis_index_groups=team_sets)

    def spread(values):
        if paired:
            values = team(values.reshape(2, 2, count, local_width), 1, 0)
        values = values.reshape(cols, count, local_width)
        return lax.all_to_all(values, "cols", 0, 1).reshape(count, width)

    def collect(values):
        values = lax.all_to_all(values.reshape(count, cols, local_width), "cols", 1, 0)
        if paired:
            values = team(values.reshape(2, 2, count, local_width), 0, 1)
        return values.reshape(length, local_width)

    def to_heads(values):
        part = values.shape[1] // share
        return team(values.reshape(count, share, part), 1, 0).reshape(share * count, part)

    def to_tokens(values):
        part = values.shape[1]
        return team(values.reshape(share, count, part), 0, 1).reshape(count, share * part)

    def gather_in(weight):
        weight = lax.all_gather(weight, "cols", axis=weight.ndim - 1, tiled=True)
        return lax.all_gather(weight, "rows", axis=0, tiled=True)

    def gather_out(weight):
        weight = lax.all_gather(weight, "cols", axis=0, tiled=True)
        return lax.all_gather(weight, "rows", axis=1, tiled=True)

    def scatter_in(grad):
        grad = grad.astype(BF16)
        grad = lax.psum_scatter(grad, "rows", scatter_dimension=0, tiled=True)
        grad = lax.psum_scatter(grad, "cols", scatter_dimension=grad.ndim - 1, tiled=True)
        return grad.astype(F32)

    def scatter_out(grad):
        grad = grad.astype(BF16)
        grad = lax.psum_scatter(grad, "rows", scatter_dimension=1, tiled=True)
        grad = lax.psum_scatter(grad, "cols", scatter_dimension=0, tiled=True)
        return grad.astype(F32)

    segment = segment_ids[0]
    member = segment[:, None] == jnp.arange(DOCS, dtype=jnp.int32)[None, :]
    sizes = jnp.sum(member.astype(jnp.int32), axis=0, dtype=jnp.int32)
    starts = jnp.cumsum(sizes, dtype=jnp.int32) - sizes
    doc_start = jnp.sum(jnp.where(member, starts[None, :], 0), axis=1, dtype=jnp.int32)
    position = jnp.arange(length, dtype=jnp.int32) - doc_start
    turn = jnp.sum(jnp.where(sizes == length // 2, starts, 0), dtype=jnp.int32)
    position = jnp.roll(position, -turn)
    if paired:
        both = lax.all_gather(position, "rows", axis_index_groups=team_sets)
        halves = both.reshape(cols, length // 2)
        which = lax.axis_index("cols")
    else:
        halves = position.reshape(2, length // 2)
        which = lax.axis_index("cols") // share
    half = lax.dynamic_index_in_dim(halves, which, 0, keepdims=False)
    start = jnp.arange(length // 2, dtype=jnp.int32) - half
    own = lax.dynamic_slice_in_dim(half, seat * count, count).astype(F32)
    frequency = THETA ** (-jnp.arange(0, HEAD, 2, dtype=F32) / HEAD)
    angles = own[:, None] * frequency[None, :]
    cosine, sine_table = jnp.cos(angles), jnp.sin(angles)
    block = min(BLOCK, length // 2)

    x = spread(jnp.roll(tokens, -turn, axis=0)).astype(F32)
    w_qkv = gather_in(qkv_weight)
    w_out = gather_out(out_weight)
    w_expand = gather_in(expand_weight)
    w_down = gather_out(down_weight)
    grad_low = spread(jnp.roll(cotangent, -turn, axis=0))

    scale_one = norm_scale(x)
    normed_one = (x * scale_one * attn_gain).astype(BF16)
    grouped = dot(normed_one, w_qkv, 1, 0).reshape(count, KV_HEADS, PER + 2, HEAD)
    query_raw = grouped[:, :, :PER]
    key_raw = grouped[:, :, PER]
    local_heads = partial(heads_local, cosine=cosine, sine_table=sine_table)
    (queries, keys), pullback = jax.vjp(local_heads, query_raw, key_raw, query_gain, key_gain)
    packed = jnp.concatenate(
        [queries.astype(BF16), keys.astype(BF16)[:, :, None], grouped[:, :, PER + 1 :].astype(BF16)],
        axis=2,
    )
    qkv = to_heads(packed.reshape(count, KV_HEADS * WIDTH))
    mixed_heads, lse = attend(qkv, start, block)
    mixed = to_tokens(mixed_heads)

    hidden = x + dot(mixed, w_out, 1, 0)
    scale_two = norm_scale(hidden)
    normed_two = (hidden * scale_two * mlp_gain).astype(BF16)
    gate_up = jnp.einsum("tk,ksf->tsf", normed_two, w_expand, preferred_element_type=F32)
    gate = gate_up[:, 0]
    upper = gate_up[:, 1]
    sigmoid_gate = jax.nn.sigmoid(gate)
    silu_gate = gate * sigmoid_gate
    activation = (silu_gate * upper).astype(BF16)
    output = collect((hidden + dot(activation, w_down, 1, 0)).astype(BF16))
    output = jnp.roll(output, turn, axis=0)

    act_grad = dot(grad_low, w_down, 1, 1)
    down_grad = scatter_out(dot(activation, grad_low, 0, 0))
    gate_grad = act_grad * upper * sigmoid_gate * (1.0 + gate * (1.0 - sigmoid_gate))
    upper_grad = act_grad * silu_gate
    expand_back = jnp.stack([gate_grad, upper_grad], axis=1).astype(BF16)
    normed_grad_two = jnp.einsum("tsf,ksf->tk", expand_back, w_expand, preferred_element_type=F32)
    expand_grad = scatter_in(
        jnp.einsum("tk,tsf->ksf", normed_two, expand_back, preferred_element_type=F32)
    )
    back_two, gain_two_grad = norm_backward(hidden, scale_two, mlp_gain, normed_grad_two)
    hidden_grad = grad_low.astype(F32) + back_two
    hidden_low = hidden_grad.astype(BF16)
    mixed_grad = to_heads(dot(hidden_low, w_out, 1, 1).astype(BF16))
    out_grad = scatter_out(dot(mixed, hidden_low, 0, 0))

    back = to_tokens(attend_back(qkv, mixed_heads, lse, mixed_grad, start, block))
    back = back.reshape(count, KV_HEADS, PER + 2, HEAD)
    query_raw_grad, key_raw_grad, query_gain_part, key_gain_part = pullback(
        (back[:, :, :PER].astype(F32), back[:, :, PER].astype(F32))
    )
    qkv_back = jnp.concatenate(
        [
            query_raw_grad.astype(BF16),
            key_raw_grad.astype(BF16)[:, :, None],
            back[:, :, PER + 1 :],
        ],
        axis=2,
    ).reshape(count, KV_HEADS * WIDTH)
    normed_grad_one = dot(qkv_back, w_qkv, 1, 1)
    qkv_grad = scatter_in(dot(normed_one, qkv_back, 0, 0))
    back_one, gain_one_grad = norm_backward(x, scale_one, attn_gain, normed_grad_one)
    input_grad = collect((hidden_grad + back_one).astype(BF16))
    input_grad = jnp.roll(input_grad, turn, axis=0).astype(F32)
    gains = lax.psum(
        jnp.concatenate([gain_one_grad, gain_two_grad, query_gain_part, key_gain_part]),
        ("rows", "cols"),
    )
    return (
        output,
        input_grad,
        qkv_grad,
        out_grad,
        expand_grad,
        down_grad,
        gains[:width],
        gains[width : 2 * width],
        gains[2 * width : 2 * width + HEAD],
        gains[2 * width + HEAD :],
    )


def solution(mesh):
    return jax.shard_map(
        local,
        mesh=mesh,
        in_specs=(
            P("rows", "cols"),
            P("rows", "cols"),
            P("cols", "rows"),
            P("rows", None, "cols"),
            P("cols", "rows"),
            P(),
            P(),
            P(),
            P(),
            P("rows", None),
            P("rows", "cols"),
        ),
        out_specs=(
            P("rows", "cols"),
            P("rows", "cols"),
            P("rows", "cols"),
            P("cols", "rows"),
            P("rows", None, "cols"),
            P("cols", "rows"),
            P(),
            P(),
            P(),
            P(),
        ),
        check_vma=False,
    )
```

```python
from functools import partial

import jax
import jax.numpy as jnp
from jax import lax
from jax.experimental import pallas as pl
from jax.experimental.pallas import tpu as pltpu
from jax.sharding import PartitionSpec as P

HEADS = 16
KV_HEADS = 8
HEAD = 128
DOCS = 4
PER = HEADS // KV_HEADS
WIDTH = (PER + 2) * HEAD

EPS = 1e-06
THETA = 1000000.0
LOG2E = 1.4426950408889634
SCALE = HEAD ** (-0.5)
BLOCK = 512
F32 = jnp.float32
BF16 = jnp.bfloat16


def dot(a, b, ca, cb):
    return lax.dot_general(a, b, (((ca,), (cb,)), ((), ())), preferred_element_type=F32)


def forward_kernel(lo, full, qk_ref, k_ref, v_ref, start_ref, o_ref, lse_ref, vext, acc):
    i = pl.program_id(1)
    block = qk_ref.shape[0]

    @pl.when(i == 0)
    def _():
        vext[:, :HEAD] = v_ref[...]
        vext[:, HEAD:] = jnp.ones((vext.shape[0], HEAD), BF16)

    acc[...] = jnp.zeros_like(acc)

    def step(j, masked):
        at = pl.ds(pl.multiple_of(j * block, block), block)
        keys = k_ref[at, :]
        vals = vext[at, :]
        if masked:
            place = lax.broadcasted_iota(jnp.int32, (block, block), 1) + j * block
            query = lax.broadcasted_iota(jnp.int32, (block, block), 0) + i * block
            keep = (place >= start_ref[:, :1]) & (place <= query)
        for h in range(PER):
            s = dot(qk_ref[:, h * HEAD : (h + 1) * HEAD], keys, 1, 1)
            p = jnp.exp2(s * (SCALE * LOG2E))
            if masked:
                p = jnp.where(keep, p, 0.0)
            acc[h] += dot(p.astype(BF16), vals, 1, 0)

    first = jnp.minimum(full[i], i)

    @pl.loop(lo[i], first)
    def _(j):
        step(j, True)

    @pl.loop(first, i)
    def _(j):
        step(j, False)

    step(i, True)
    for h in range(PER):
        total = acc[h, :, HEAD:]
        o_ref[:, h * HEAD : (h + 1) * HEAD] = (acc[h, :, :HEAD] / total).astype(BF16)
        lse_ref[h] = jnp.transpose(jnp.log2(total))[:8]


def backward_kernel(
    last, full, q_ref, k_ref, v_ref, do_ref, o_ref, lse_ref, start_ref, out_ref, dq, inner, dk, dv
):
    j = pl.program_id(1)
    block = k_ref.shape[0]
    steps = pl.num_programs(1)

    @pl.when(j == 0)
    def _():
        dq[...] = jnp.zeros_like(dq)

        @pl.loop(0, steps)
        def _(i):
            at = pl.ds(pl.multiple_of(i * block, block), block)
            for h in range(PER):
                cols = slice(h * HEAD, (h + 1) * HEAD)
                term = do_ref[at, cols].astype(F32) * o_ref[at, cols].astype(F32)
                row = jnp.sum(term, axis=1, keepdims=True)
                inner[h, :, at] = jnp.transpose(jnp.broadcast_to(row, (block, HEAD)))[:8]

    dk[...] = jnp.zeros_like(dk)
    dv[...] = jnp.zeros_like(dv)
    keys = k_ref[...]
    vals = v_ref[...]

    def step(i, masked):
        at = pl.ds(pl.multiple_of(i * block, block), block)
        if masked:
            place = lax.broadcasted_iota(jnp.int32, (block, block), 0) + j * block
            query = lax.broadcasted_iota(jnp.int32, (block, block), 1) + i * block
            keep = (place >= start_ref[:1, at]) & (place <= query)
        for h in range(PER):
            cols = slice(h * HEAD, (h + 1) * HEAD)
            q = q_ref[at, cols]
            do = do_ref[at, cols]
            s = dot(keys, q, 1, 1)
            p = jnp.exp2(s * (SCALE * LOG2E) - lse_ref[h, :1, at])
            if masked:
                p = jnp.where(keep, p, 0.0)
            dp = dot(vals, do, 1, 1)
            ds = (p * (dp - inner[h, :1, at])).astype(BF16)
            dv[...] += dot(p.astype(BF16), do, 1, 0)
            dk[...] += dot(ds, q, 1, 0)
            dq[at, cols] += dot(ds, keys, 0, 0)

    step(j, True)
    middle = jnp.maximum(full[j], j) + 1

    @pl.loop(j + 1, middle)
    def _(i):
        step(i, False)

    @pl.loop(middle, last[j] + 1)
    def _(i):
        step(i, True)

    here = pl.ds(pl.multiple_of(j * block, block), block)
    out_ref[here, PER * HEAD : (PER + 1) * HEAD] = (dk[...] * SCALE).astype(BF16)
    out_ref[here, (PER + 1) * HEAD :] = dv[...].astype(BF16)

    @pl.when(j == steps - 1)
    def _():
        out_ref[:, : PER * HEAD] = (dq[...] * SCALE).astype(BF16)


def attend(qkv, start, block):
    length, width = qkv.shape
    groups = width // WIDTH
    steps = length // block
    blocked = start.reshape(steps, block)
    lo = blocked[:, 0] // block
    full = (blocked[:, -1] + block - 1) // block
    wide = jnp.broadcast_to(start[:, None], (length, HEAD))
    return pl.pallas_call(
        forward_kernel,
        grid_spec=pltpu.PrefetchScalarGridSpec(
            num_scalar_prefetch=2,
            grid=(groups, steps),
            in_specs=[
                pl.BlockSpec((block, PER * HEAD), lambda g, i, *_: (i, g * 2)),
                pl.BlockSpec((length, HEAD), lambda g, i, *_: (0, g * 4 + 2)),
                pl.BlockSpec((length, HEAD), lambda g, i, *_: (0, g * 4 + 3)),
                pl.BlockSpec((block, HEAD), lambda g, i, *_: (i, 0)),
            ],
            out_specs=[
                pl.BlockSpec((block, PER * HEAD), lambda g, i, *_: (i, g)),
                pl.BlockSpec((PER, 8, block), lambda g, i, *_: (g, 0, i)),
            ],
            scratch_shapes=[
                pltpu.VMEM((length, 2 * HEAD), BF16),
                pltpu.VMEM((PER, block, 2 * HEAD), F32),
            ],
        ),
        out_shape=[
            jax.ShapeDtypeStruct((length, groups * PER * HEAD), BF16),
            jax.ShapeDtypeStruct((groups * PER, 8, length), F32),
        ],
        compiler_params=pltpu.CompilerParams(vmem_limit_bytes=40 * 2**20),
        cost_estimate=pl.CostEstimate(
            flops=groups * PER * length * length * HEAD * 4,
            bytes_accessed=length * width * 4,
            transcendentals=groups * PER * length * length // 2,
        ),
        name="attend",
    )(lo, full, qkv, qkv, qkv, wide)


def attend_back(qkv, mixed, lse, grad, start, block):
    length, width = qkv.shape
    groups = width // WIDTH
    steps = length // block
    blocked = start.reshape(steps, block)
    index = jnp.arange(steps, dtype=jnp.int32)
    last = jnp.sum((blocked[:, 0] // block)[None, :] <= index[:, None], axis=1, dtype=jnp.int32) - 1
    full = jnp.sum(blocked[:, -1][None, :] <= (index * block)[:, None], axis=1, dtype=jnp.int32) - 1
    wide = jnp.broadcast_to(start[None, :], (8, length))
    return pl.pallas_call(
        backward_kernel,
        grid_spec=pltpu.PrefetchScalarGridSpec(
            num_scalar_prefetch=2,
            grid=(groups, steps),
            in_specs=[
                pl.BlockSpec((length, PER * HEAD), lambda g, j, *_: (0, g * 2)),
                pl.BlockSpec((block, HEAD), lambda g, j, *_: (j, g * 4 + 2)),
                pl.BlockSpec((block, HEAD), lambda g, j, *_: (j, g * 4 + 3)),
                pl.BlockSpec((length, PER * HEAD), lambda g, j, *_: (0, g)),
                pl.BlockSpec((length, PER * HEAD), lambda g, j, *_: (0, g)),
                pl.BlockSpec((PER, 8, length), lambda g, j, *_: (g, 0, 0)),
                pl.BlockSpec((8, length), lambda g, j, *_: (0, 0)),
            ],
            out_specs=pl.BlockSpec((length, WIDTH), lambda g, j, *_: (0, g)),
            scratch_shapes=[
                pltpu.VMEM((length, PER * HEAD), F32),
                pltpu.VMEM((PER, 8, length), F32),
                pltpu.VMEM((block, HEAD), F32),
                pltpu.VMEM((block, HEAD), F32),
            ],
        ),
        out_shape=jax.ShapeDtypeStruct((length, width), BF16),
        compiler_params=pltpu.CompilerParams(vmem_limit_bytes=48 * 2**20),
        cost_estimate=pl.CostEstimate(
            flops=groups * PER * length * length * HEAD * 10,
            bytes_accessed=length * width * 8,
            transcendentals=groups * PER * length * length // 2,
        ),
        name="attend_back",
    )(last, full, qkv, qkv, qkv, grad, mixed, lse, wide)


def rotate(values, cosine, sine_table):
    half_size = values.shape[-1] // 2
    front = values[..., :half_size]
    back_half = values[..., half_size:]
    return jnp.concatenate(
        [front * cosine - back_half * sine_table, back_half * cosine + front * sine_table], axis=-1
    )


def head_norm(values, scaling):
    return values * lax.rsqrt(jnp.mean(values * values, axis=-1, keepdims=True) + EPS) * scaling


def heads_local(query_raw, key_raw, query_gain, key_gain, cosine, sine_table):
    queries = rotate(
        head_norm(query_raw, query_gain), cosine[:, None, None], sine_table[:, None, None]
    )
    keys = rotate(head_norm(key_raw, key_gain), cosine[:, None], sine_table[:, None])
    return (queries, keys)


def norm_scale(values):
    return lax.rsqrt(jnp.mean(values * values, axis=1, keepdims=True) + EPS)


def norm_backward(values, scale, scaling, gradient):
    inner_sum = jnp.mean(gradient * scaling * values, axis=1, keepdims=True)
    back_grad = scale * scaling * gradient - values * scale * scale * scale * inner_sum
    gain_part = jnp.sum(gradient * values * scale, axis=0)
    return (back_grad, gain_part)


def local(
    tokens,
    qkv_weight,
    out_weight,
    expand_weight,
    down_weight,
    attn_gain,
    mlp_gain,
    query_gain,
    key_gain,
    segment_ids,
    cotangent,
):
    rows = lax.axis_size("rows")
    cols = lax.axis_size("cols")
    length, local_width = tokens.shape
    width = local_width * cols
    paired = cols == 4 and rows % 2 == 0
    share = 2 if paired else cols // 2
    count = length // cols
    if paired:
        team_axis = "rows"
        team_sets = [[2 * i, 2 * i + 1] for i in range(rows // 2)]
        seat = lax.axis_index("rows") % 2
    else:
        team_axis = "cols"
        team_sets = [[share * i + k for k in range(share)] for i in range(2)]
        seat = lax.axis_index("cols") % share

    def team(values, split, concat):
        return lax.all_to_all(values, team_axis, split, concat, axis_index_groups=team_sets)

    def spread(values):
        if paired:
            values = team(values.reshape(2, 2, count, local_width), 1, 0)
        values = values.reshape(cols, count, local_width)
        return lax.all_to_all(values, "cols", 0, 1).reshape(count, width)

    def collect(values):
        values = lax.all_to_all(values.reshape(count, cols, local_width), "cols", 1, 0)
        if paired:
            values = team(values.reshape(2, 2, count, local_width), 0, 1)
        return values.reshape(length, local_width)

    def to_heads(values):
        part = values.shape[1] // share
        return team(values.reshape(count, share, part), 1, 0).reshape(share * count, part)

    def to_tokens(values):
        part = values.shape[1]
        return team(values.reshape(share, count, part), 0, 1).reshape(count, share * part)

    def gather_in(weight):
        weight = lax.all_gather(weight, "cols", axis=weight.ndim - 1, tiled=True)
        return lax.all_gather(weight, "rows", axis=0, tiled=True)

    def gather_out(weight):
        weight = lax.all_gather(weight, "rows", axis=1, tiled=True)
        return lax.all_gather(weight, "cols", axis=0, tiled=True)

    def rows_in(grad):
        return lax.psum_scatter(grad, "rows", scatter_dimension=0, tiled=True)

    def cols_in(grad):
        grad = lax.psum_scatter(grad, "cols", scatter_dimension=grad.ndim - 1, tiled=True)
        return grad.astype(F32)

    def rows_out(grad):
        return lax.psum_scatter(grad, "rows", scatter_dimension=1, tiled=True)

    def cols_out(grad):
        grad = lax.psum_scatter(grad, "cols", scatter_dimension=0, tiled=True)
        return grad.astype(F32)

    segment = segment_ids[0]
    member = segment[:, None] == jnp.arange(DOCS, dtype=jnp.int32)[None, :]
    sizes = jnp.sum(member.astype(jnp.int32), axis=0, dtype=jnp.int32)
    starts = jnp.cumsum(sizes, dtype=jnp.int32) - sizes
    doc_start = jnp.sum(jnp.where(member, starts[None, :], 0), axis=1, dtype=jnp.int32)
    position = jnp.arange(length, dtype=jnp.int32) - doc_start
    turn = jnp.sum(jnp.where(sizes == length // 2, starts, 0), dtype=jnp.int32)
    position = jnp.roll(position, -turn)
    if paired:
        both = lax.all_gather(position, "rows", axis_index_groups=team_sets)
        halves = both.reshape(cols, length // 2)
        which = lax.axis_index("cols")
    else:
        halves = position.reshape(2, length // 2)
        which = lax.axis_index("cols") // share
    half = lax.dynamic_index_in_dim(halves, which, 0, keepdims=False)
    start = jnp.arange(length // 2, dtype=jnp.int32) - half
    own = lax.dynamic_slice_in_dim(half, seat * count, count).astype(F32)
    frequency = THETA ** (-jnp.arange(0, HEAD, 2, dtype=F32) / HEAD)
    angles = own[:, None] * frequency[None, :]
    cosine, sine_table = jnp.cos(angles), jnp.sin(angles)
    block = min(BLOCK, length // 2)

    w_qkv = gather_in(qkv_weight)
    x_low = spread(jnp.roll(tokens, -turn, axis=0))
    x_low, out_weight, expand_weight, down_weight = lax.optimization_barrier(
        (x_low, out_weight, expand_weight, down_weight)
    )
    x = x_low.astype(F32)
    w_out = gather_out(out_weight)
    w_expand = gather_in(expand_weight)
    w_down = gather_out(down_weight)
    grad_low = spread(jnp.roll(cotangent, -turn, axis=0))

    scale_one = norm_scale(x)
    normed_one = (x * scale_one * attn_gain).astype(BF16)
    grouped = dot(normed_one, w_qkv, 1, 0).reshape(count, KV_HEADS, PER + 2, HEAD)
    query_raw = grouped[:, :, :PER]
    key_raw = grouped[:, :, PER]
    local_heads = partial(heads_local, cosine=cosine, sine_table=sine_table)
    (queries, keys), pullback = jax.vjp(local_heads, query_raw, key_raw, query_gain, key_gain)
    packed = jnp.concatenate(
        [queries.astype(BF16), keys.astype(BF16)[:, :, None], grouped[:, :, PER + 1 :].astype(BF16)],
        axis=2,
    )
    qkv = to_heads(packed.reshape(count, KV_HEADS * WIDTH))
    mixed_heads, lse = attend(qkv, start, block)
    mixed = to_tokens(mixed_heads)

    hidden = x + dot(mixed, w_out, 1, 0)
    scale_two = norm_scale(hidden)
    normed_two = (hidden * scale_two * mlp_gain).astype(BF16)
    gate_up = jnp.einsum("tk,ksf->tsf", normed_two, w_expand, preferred_element_type=F32)
    gate = gate_up[:, 0]
    upper = gate_up[:, 1]
    sigmoid_gate = jax.nn.sigmoid(gate)
    silu_gate = gate * sigmoid_gate
    activation = (silu_gate * upper).astype(BF16)
    result = (hidden + dot(activation, w_down, 1, 0)).astype(BF16)

    act_grad = dot(grad_low, w_down, 1, 1)
    down_part = dot(activation, grad_low, 0, 0).astype(BF16)
    gate_grad = act_grad * upper * sigmoid_gate * (1.0 + gate * (1.0 - sigmoid_gate))
    upper_grad = act_grad * silu_gate
    expand_back = jnp.stack([gate_grad, upper_grad], axis=1).astype(BF16)
    normed_grad_two = jnp.einsum("tsf,ksf->tk", expand_back, w_expand, preferred_element_type=F32)
    expand_part = jnp.einsum(
        "tk,tsf->ksf", normed_two, expand_back, preferred_element_type=F32
    ).astype(BF16)
    normed_grad_two, down_part, expand_part = lax.optimization_barrier(
        (normed_grad_two, down_part, expand_part)
    )
    expand_part = rows_in(expand_part)
    down_part = rows_out(down_part)
    back_two, gain_two_grad = norm_backward(hidden, scale_two, mlp_gain, normed_grad_two)
    hidden_grad = grad_low.astype(F32) + back_two
    hidden_low = hidden_grad.astype(BF16)
    mixed_grad, out_part, result = lax.optimization_barrier(
        (
            dot(hidden_low, w_out, 1, 1).astype(BF16),
            dot(mixed, hidden_low, 0, 0).astype(BF16),
            result,
        )
    )
    output = collect(result)
    mixed_grad = to_heads(mixed_grad)
    out_grad = cols_out(rows_out(out_part))

    back = attend_back(qkv, mixed_heads, lse, mixed_grad, start, block)
    back, output, expand_part, down_part = lax.optimization_barrier(
        (back, output, expand_part, down_part)
    )
    expand_grad = cols_in(expand_part)
    down_grad = cols_out(down_part)
    output = jnp.roll(output, turn, axis=0)
    back = to_tokens(back)
    back = back.reshape(count, KV_HEADS, PER + 2, HEAD)
    query_raw_grad, key_raw_grad, query_gain_part, key_gain_part = pullback(
        (back[:, :, :PER].astype(F32), back[:, :, PER].astype(F32))
    )
    qkv_back = jnp.concatenate(
        [
            query_raw_grad.astype(BF16),
            key_raw_grad.astype(BF16)[:, :, None],
            back[:, :, PER + 1 :],
        ],
        axis=2,
    ).reshape(count, KV_HEADS * WIDTH)
    normed_grad_one = dot(qkv_back, w_qkv, 1, 1)
    qkv_grad = cols_in(rows_in(dot(normed_one, qkv_back, 0, 0).astype(BF16)))
    back_one, gain_one_grad = norm_backward(x, scale_one, attn_gain, normed_grad_one)
    input_grad = collect((hidden_grad + back_one).astype(BF16))
    input_grad = jnp.roll(input_grad, turn, axis=0).astype(F32)
    gains = lax.psum(
        jnp.concatenate([gain_one_grad, gain_two_grad, query_gain_part, key_gain_part]),
        ("rows", "cols"),
    )
    return (
        output,
        input_grad,
        qkv_grad,
        out_grad,
        expand_grad,
        down_grad,
        gains[:width],
        gains[width : 2 * width],
        gains[2 * width : 2 * width + HEAD],
        gains[2 * width + HEAD :],
    )


def solution(mesh):
    return jax.shard_map(
        local,
        mesh=mesh,
        in_specs=(
            P("rows", "cols"),
            P("rows", "cols"),
            P("cols", "rows"),
            P("rows", None, "cols"),
            P("cols", "rows"),
            P(),
            P(),
            P(),
            P(),
            P("rows", None),
            P("rows", "cols"),
        ),
        out_specs=(
            P("rows", "cols"),
            P("rows", "cols"),
            P("rows", "cols"),
            P("cols", "rows"),
            P("rows", None, "cols"),
            P("cols", "rows"),
            P(),
            P(),
            P(),
            P(),
        ),
        check_vma=False,
    )
```
